256 devices in a mesh: pb: 8 (over y_hi, x), mem: 32 (over y_lo, z, core).
Axes of the slice: x: 4, y: 4 (y_hi: 2, y_lo: 2; y = y_hi * 2 + y_lo), z: 8, core: 2. Of those that a mesh axis runs over, the one named last changes fastest.
Arguments:
- queries: bfloat16 [2048, 2048], P('pb'), may hold values from -12 to 12
- keys: bfloat16 [32768, 2048], P('mem'), may hold values from -12 to 12
- values: bfloat16 [32768, 2048], P('mem'), may hold values from -6 to 6
- d_out: bfloat16 [2048, 2048], P('pb'), may hold values from -6 to 6
Outputs:
- query_grad: float32 [2048, 2048], P(('pb', 'mem'))
- key_grad: bfloat16 [32, 1024, 2048], P('mem', 'pb')
- value_grad: bfloat16 [32, 1024, 2048], P('mem', 'pb')
The draws below stay inside these ranges and needn't reach their ends.
All inputs are finite; a program needn't handle non-finite values.
Results may differ from the reference program's by a relative error of at most 0.022.
Values may be sent and summed in bfloat16 or wider, within the bound.
A program may use at most 192 MiB of HBM per device.

```python
import math
import jax
import jax.numpy as jnp
from jax import lax

H = 16
DH = 128
MEM_DEV = 1024
HD = 2048
S = 2048
MEM_SLOTS = 32768
N_MEM = 32


def row_scales(key, lowest, ratio):
    uniform_part = jax.random.uniform(key, (S, 1), jnp.float32)
    return lowest * jnp.exp(uniform_part * math.log(ratio))


def draw_queries(key, part):
    key = jax.random.fold_in(key, 11)
    scale_key = jax.random.fold_in(key, 5)
    row_scale = row_scales(scale_key, 0.25, 24.0)
    base = jnp.clip(row_scale * jax.random.normal(key, (S, HD), jnp.float32), -11.0, 11.0)
    return base.astype(jnp.bfloat16)


def draw_keys(key, part):
    key = jax.random.fold_in(key, 23)
    base = jnp.clip(jax.random.normal(key, (MEM_SLOTS, HD), jnp.float32), -4.5, 4.5)
    return base.astype(jnp.bfloat16)


def block_levels(own_key, extent, split, least, top_value):
    def one(dim, blocks):
        draws = jax.random.uniform(jax.random.fold_in(jax.random.fold_in(own_key, 6), dim), (blocks,), jnp.float32, least / len(split), top_value / len(split))
        return jnp.repeat(jnp.exp(draws), extent[dim] // blocks).reshape((-1,) + (1,) * (len(extent) - dim - 1))

    level = one(*split[0])
    for cut in split[1:]:
        level = level * one(*cut)
    return level


def normal_values(key, shape, spread, most, cuts=(), kind=jnp.bfloat16):
    values = spread * jax.random.normal(key, shape, jnp.float32)
    if cuts:
        values = values * block_levels(key, shape, cuts, -0.22, 0.18)
    return jnp.clip(values, -most, most).astype(kind)


def setup_inputs(seed: int = 0) -> dict:
    streams_of = jax.random.split(jax.random.key(seed), 5)
    return {
        "queries": draw_queries(jax.random.fold_in(streams_of[4], 71), 0),
        "keys": draw_keys(jax.random.fold_in(streams_of[4], 71), 0),
        "values": normal_values(streams_of[2], (MEM_SLOTS, HD), 1.0, 6.0, ((0, 32),)),
        "d_out": normal_values(streams_of[3], (S, HD), 1.0, 6.0, ((0, 8),)),
    }


def reference(queries, keys, values, d_out):
    scale = DH ** -0.5
    q3 = queries.astype(jnp.float32).reshape(S, H, DH)
    do3 = d_out.astype(jnp.float32).reshape(S, H, DH)
    blk = math.gcd(MEM_SLOTS, 2048)
    nblk = MEM_SLOTS // blk
    key_blocks = keys.reshape(nblk, blk, H, DH)
    value_blocks = values.reshape(nblk, blk, H, DH)

    def scored(kb):
        return jnp.einsum("rhd,jhd->hrj", q3, kb.astype(jnp.float32)) * scale

    row_max = lax.map(lambda kb: jnp.max(scored(kb), axis=-1), key_blocks).max(axis=0)
    row_total = lax.map(lambda kb: jnp.sum(jnp.exp(scored(kb) - row_max[:, :, None]), axis=-1), key_blocks).sum(axis=0)

    def weights(kb):
        return (jnp.exp(scored(kb) - row_max[:, :, None]) / row_total[:, :, None]).astype(jnp.bfloat16)

    def attend(pair):
        return jnp.einsum("hrj,jhd->rhd", weights(pair[0]).astype(jnp.float32), pair[1].astype(jnp.float32))

    attended = lax.map(attend, (key_blocks, value_blocks)).sum(axis=0)
    row_term = jnp.sum(do3 * attended, axis=-1).T

    def grads(pair):
        kb = pair[0].astype(jnp.float32)
        vb = pair[1].astype(jnp.float32)
        probs = weights(pair[0])
        dprobs = jnp.einsum("rhd,jhd->hrj", do3, vb)
        dscores = (probs.astype(jnp.float32) * (dprobs - row_term[:, :, None])).astype(jnp.bfloat16).astype(jnp.float32)
        dq_part = jnp.einsum("hrj,jhd->rhd", dscores, kb)
        dk_part = jnp.einsum("hrj,rhd->jhd", dscores, q3)
        dv_part = jnp.einsum("hrj,rhd->jhd", probs.astype(jnp.float32), do3)
        return dq_part, dk_part, dv_part

    dq_parts, dk_parts, dv_parts = lax.map(grads, (key_blocks, value_blocks))
    query_grad = (scale * dq_parts.sum(axis=0)).reshape(S, HD)
    key_grad = (scale * dk_parts).astype(jnp.bfloat16).reshape(N_MEM, MEM_DEV, HD)
    value_grad = dv_parts.astype(jnp.bfloat16).reshape(N_MEM, MEM_DEV, HD)
    return query_grad, key_grad, value_grad
```

```python
import functools
import math

import jax
import jax.numpy as jnp
from jax import lax
from jax.experimental import pallas as pl
from jax.experimental.pallas import tpu as pltpu
from jax.sharding import PartitionSpec as P

MESH = pl.DeviceIdType.MESH
DH = 128
NB = 8
NG = 16
RB = 256
KB = 1024
KP = 128
KT = 256
SCALE = DH ** -0.5
C2 = SCALE * math.log2(math.e)
F32 = jnp.float32
BF16 = jnp.bfloat16


def kernel(
    q_hbm, k_hbm, v_hbm, do_hbm, dq_out, dk_out, dv_out,
    qb, dob, kb, vb, kt, sc, dp, st, sr, rs, rr, dka, dva, dks, dvs, dqa, dqs, dqr, dqo,
    l_sem, kv_send, kv_recv, in_send, in_recv, st_send, st_recv, bc_send, bc_recv,
    o_send, o_recv, dq_send, dq_recv, f_send, f_recv,
):
    p = lax.axis_index("pb")
    m = lax.axis_index("mem")
    yh, x = p // 4, p % 4
    g, c = m // 2, m % 2
    head = 2 * p + c

    def cols(h):
        return pl.ds(pl.multiple_of(h * DH, DH), DH)

    def source(r):
        return (yh + r // 4) % 2 * 4 + (x + r) % 4

    def target(r):
        return (yh + r // 4) % 2 * 4 + (x + 4 - r % 4) % 4

    def local(src, dst, sem):
        pltpu.make_async_copy(src, dst, sem).start()

    def remote(src, dst, send, recv, pb, mem):
        pltpu.make_async_remote_copy(
            src_ref=src, dst_ref=dst, send_sem=send, recv_sem=recv,
            device_id=(pb, mem), device_id_type=MESH,
        ).start()

    def settle(ref, sem):
        pltpu.make_async_copy(ref, ref, sem).wait()

    local(k_hbm.at[:, cols(head)], kb.at[0], l_sem.at[0])
    local(v_hbm.at[:, cols(head)], vb.at[0], l_sem.at[1])
    local(q_hbm.at[:, cols(head)], qb.at[0], in_recv.at[0, 0])
    local(do_hbm.at[:, cols(head)], dob.at[0], in_recv.at[0, 1])

    barrier = pltpu.get_barrier_semaphore()

    @pl.loop(1, 2 * NB)
    def _(i):
        pl.semaphore_signal(
            barrier, inc=1, device_id=((p + i // 2) % NB, 2 * g + (c + i) % 2), device_id_type=MESH
        )

    @pl.loop(1, NG)
    def _(i):
        pl.semaphore_signal(
            barrier, inc=1, device_id=(p, (g + i) % NG * 2 + c), device_id_type=MESH
        )

    pl.semaphore_wait(barrier, 2 * NB + NG - 2)

    mate = 2 * p + 1 - c
    remote(k_hbm.at[:, cols(mate)], kb.at[1], kv_send, kv_recv, p, 2 * g + 1 - c)
    remote(v_hbm.at[:, cols(mate)], vb.at[1], kv_send, kv_recv, p, 2 * g + 1 - c)

    @pl.loop(1, NB)
    def _(r):
        to = target(r)
        remote(q_hbm.at[:, cols(2 * to + c)], qb.at[r], in_send.at[0], in_recv.at[r, 0], to, m)
        remote(do_hbm.at[:, cols(2 * to + c)], dob.at[r], in_send.at[1], in_recv.at[r, 1], to, m)

    settle(kb.at[0], l_sem.at[0])
    settle(vb.at[0], l_sem.at[1])
    settle(kb, kv_recv)

    for half in range(2):
        kt[half] = kb[half].T

    def combine(tile):
        @pl.when(g // 2 == tile)
        def _():
            settle(sr, st_recv)
            tm, tl, tt = sr[:, 0, :], sr[:, 1, :], sr[:, 2, :]
            top = jnp.max(tm, axis=0, keepdims=True)
            w = jnp.exp2((tm - top) * C2)
            total = jnp.sum(tl * w, axis=0, keepdims=True)
            term = jnp.sum(tt * w, axis=0, keepdims=True) / total
            rs[...] = jnp.concatenate([top * C2 + jnp.log2(total), term, jnp.zeros((6, 128), F32)], axis=0)
            local(rs, rr.at[g], bc_recv.at[g])

            @pl.loop(1, NG)
            def _(i):
                remote(rs, rr.at[g], bc_send, bc_recv.at[g], p, (g + i) % NG * 2 + c)

    def forward(r, carry):
        settle(qb.at[r], in_recv.at[r, 0])
        settle(dob.at[r], in_recv.at[r, 1])
        q = qb[r]
        do = dob[r]
        top = jnp.full((8, RB), -1e30, F32)
        total = jnp.zeros((8, RB), F32)
        term = jnp.zeros((8, RB), F32)
        for half in range(2):
            for j in range(KB // KT):
                rows = pl.ds(j * KT, KT)
                s = lax.dot_general(kb[half, rows, :], q, (((1,), (1,)), ((), ())), preferred_element_type=F32)
                d = lax.dot_general(vb[half, rows, :], do, (((1,), (1,)), ((), ())), preferred_element_type=F32)
                sc[r, half, rows, :] = s
                dp[r, half, rows, :] = d
                s = s.reshape(KT // 8, 8, RB)
                d = d.reshape(KT // 8, 8, RB)
                new = jnp.maximum(top, jnp.max(s, axis=0))
                w = jnp.exp2((top - new) * C2)
                e = jnp.exp2((s - new[None]) * C2)
                total = total * w + jnp.sum(e, axis=0)
                term = term * w + jnp.sum(e * d, axis=0)
                top = new
        peak = jnp.max(top, axis=0, keepdims=True)
        w = jnp.exp2((top - peak) * C2)
        total = jnp.sum(total * w, axis=0, keepdims=True)
        term = jnp.sum(term * w, axis=0, keepdims=True)
        for k in range(2):
            lanes = slice(k * 128, k * 128 + 128)
            tile = 2 * r + k
            st[tile] = jnp.concatenate(
                [peak[:, lanes], total[:, lanes], term[:, lanes], jnp.zeros((5, 128), F32)], axis=0
            )

            @pl.when(g == tile)
            def _():
                local(st.at[tile], sr.at[g], st_recv)

            @pl.when(g != tile)
            def _():
                remote(st.at[tile], sr.at[g], st_send, st_recv, p, tile * 2 + c)

        combine(r - 2)
        return carry

    lax.fori_loop(0, NB, forward, 0)

    def backward(half, r):
        if half == 0:
            settle(rr.at[2 * r], bc_recv.at[2 * r])
            settle(rr.at[2 * r + 1], bc_recv.at[2 * r + 1])
        b = jnp.concatenate([rr[2 * r, 0:1, :], rr[2 * r + 1, 0:1, :]], axis=1)
        t = jnp.concatenate([rr[2 * r, 1:2, :], rr[2 * r + 1, 1:2, :]], axis=1)
        q = qb[r]
        do = dob[r]
        dq = jnp.zeros((DH, RB), F32)
        for j in range(KB // KT):
            rows = pl.ds(j * KT, KT)
            pr = jnp.exp2(sc[r, half, rows, :] * C2 - b)
            ds = (pr * (dp[r, half, rows, :] - t)).astype(BF16)
            pr = pr.astype(BF16)
            dva[rows, :] += jnp.dot(pr, do, preferred_element_type=F32)
            dka[rows, :] += jnp.dot(ds, q, preferred_element_type=F32)
            dq += jnp.dot(kt[half, :, rows], ds, preferred_element_type=F32)
        return dq

    def ship(half):
        dks[half * NB:(half + 1) * NB] = (dka[...] * SCALE).astype(BF16).reshape(NB, KP, DH)
        dvs[half * NB:(half + 1) * NB] = dva[...].astype(BF16).reshape(NB, KP, DH)
        to_c = 2 * g + (c + half) % 2
        if half == 0:
            local(dks.at[p], dk_out.at[:, cols(head)], o_recv.at[0])
            local(dvs.at[p], dv_out.at[:, cols(head)], o_recv.at[1])
        else:
            remote(dks.at[NB + p], dk_out.at[:, cols(head)], o_send.at[0], o_recv.at[0], p, to_c)
            remote(dvs.at[NB + p], dv_out.at[:, cols(head)], o_send.at[1], o_recv.at[1], p, to_c)

        @pl.loop(1, NB)
        def _(r):
            to = target(r)
            remote(dks.at[half * NB + to], dk_out.at[:, cols(head)], o_send.at[0], o_recv.at[0], to, to_c)
            remote(dvs.at[half * NB + to], dv_out.at[:, cols(head)], o_send.at[1], o_recv.at[1], to, to_c)

    dka[...] = jnp.zeros_like(dka)
    dva[...] = jnp.zeros_like(dva)

    def first(r, carry):
        dqa[r] = backward(0, r)
        combine(r + NB - 2)
        return carry

    lax.fori_loop(0, NB, first, 0)
    ship(0)
    dka[...] = jnp.zeros_like(dka)
    dva[...] = jnp.zeros_like(dva)

    def second(i, carry):
        for k in range(2):
            r = 2 * i + k
            dq = (backward(1, r) + dqa[r]) * SCALE
            dqs[i, :, k] = dq.T.astype(BF16).reshape(NG, RB // NG, DH)
        local(dqs.at[i, g], dqr.at[i, g], dq_recv.at[i])

        @pl.loop(1, NG)
        def _(n):
            to = (g + n) % NG
            remote(dqs.at[i, to], dqr.at[i, g], dq_send, dq_recv.at[i], p, to * 2 + c)

        return carry

    lax.fori_loop(0, NB // 2, second, 0)
    ship(1)

    for i in range(NB // 2):
        settle(dqr.at[i], dq_recv.at[i])
        for k in range(2):
            r = 2 * i + k
            acc = jnp.sum(dqr[i, :, k].astype(F32), axis=0)
            dqo[2 * r:2 * r + 2] = acc.reshape(2, 8, DH)
            to = source(r)
            for e in range(2):
                dst = dq_out.at[:, cols(head)]
                if r == 0 and e == 0:
                    local(dqo.at[c], dst, f_recv)
                else:
                    ce = (c + e) % 2
                    remote(dqo.at[2 * r + ce], dst, f_send, f_recv, to, 2 * g + ce)

    settle(dq_out, f_recv)
    settle(dk_out, o_recv.at[0])
    settle(dv_out, o_recv.at[1])
    settle(kb, kv_send)
    settle(qb.at[1:], in_send.at[0])
    settle(dob.at[1:], in_send.at[1])
    settle(st.at[1:], st_send)
    settle(rr.at[1:], bc_send)
    settle(dqs.at[:, 1:], dq_send)
    settle(dks.at[1:], o_send.at[0])
    settle(dvs.at[1:], o_send.at[1])
    settle(dqo.at[1:], f_send)


def shards(queries, keys, values, d_out):
    width = queries.shape[1]
    dma = pltpu.SemaphoreType.DMA
    return pl.pallas_call(
        kernel,
        out_shape=(
            jax.ShapeDtypeStruct((8, width), F32),
            jax.ShapeDtypeStruct((KP, width), BF16),
            jax.ShapeDtypeStruct((KP, width), BF16),
        ),
        in_specs=[pl.BlockSpec(memory_space=pl.ANY)] * 4,
        out_specs=[pl.BlockSpec(memory_space=pl.ANY)] * 3,
        scratch_shapes=[
            pltpu.VMEM((NB, RB, DH), BF16),
            pltpu.VMEM((NB, RB, DH), BF16),
            pltpu.VMEM((2, KB, DH), BF16),
            pltpu.VMEM((2, KB, DH), BF16),
            pltpu.VMEM((2, DH, KB), BF16),
            pltpu.VMEM((NB, 2, KB, RB), F32),
            pltpu.VMEM((NB, 2, KB, RB), F32),
            pltpu.VMEM((NG, 8, 128), F32),
            pltpu.VMEM((NG, 8, 128), F32),
            pltpu.VMEM((8, 128), F32),
            pltpu.VMEM((NG, 8, 128), F32),
            pltpu.VMEM((KB, DH), F32),
            pltpu.VMEM((KB, DH), F32),
            pltpu.VMEM((2 * NB, KP, DH), BF16),
            pltpu.VMEM((2 * NB, KP, DH), BF16),
            pltpu.VMEM((NB, DH, RB), F32),
            pltpu.VMEM((NB // 2, NG, 2, RB // NG, DH), BF16),
            pltpu.VMEM((NB // 2, NG, 2, RB // NG, DH), BF16),
            pltpu.VMEM((2 * NB, 8, DH), F32),
            dma((2,)),
            dma,
            dma,
            dma((2,)),
            dma((NB, 2)),
            dma,
            dma,
            dma,
            dma((NG,)),
            dma((2,)),
            dma((2,)),
            dma,
            dma((NB // 2,)),
            dma,
            dma,
        ],
        compiler_params=pltpu.CompilerParams(
            collective_id=0, has_side_effects=True, vmem_limit_bytes=56 * 2**20
        ),
        cost_estimate=pl.CostEstimate(flops=5 * 2 * 2048 * 2048 * 128, bytes_accessed=12 * 2**20, transcendentals=2 * 2048 * 2048),
    )(queries, keys, values, d_out)


def solution(mesh):
    def run(queries, keys, values, d_out):
        dq, dk, dv = shards(queries, keys, values, d_out)
        return dq, dk[None], dv[None]

    return jax.shard_map(
        run,
        mesh=mesh,
        in_specs=(P("pb", None), P("mem", None), P("mem", None), P("pb", None)),
        out_specs=(P(("pb", "mem"), None), P("mem", "pb", None), P("mem", "pb", None)),
        check_vma=False,
    )
```

```python
import functools
import math

import jax
import jax.numpy as jnp
from jax import lax
from jax.experimental import pallas as pl
from jax.experimental.pallas import tpu as pltpu
from jax.sharding import PartitionSpec as P

MESH = pl.DeviceIdType.MESH
DH = 128
NB = 8
NG = 16
RB = 256
KB = 1024
KP = 128
KT = 256
LAG = 2
BATCH = 2
ORDER = (0, 1, 3, 4, 2, 5, 7, 6)
SCALE = DH ** -0.5
C2 = SCALE * math.log2(math.e)
F32 = jnp.float32
BF16 = jnp.bfloat16


def kernel(
    q_hbm, k_hbm, v_hbm, do_hbm, dq_out, dk_out, dv_out,
    qb, dob, kb, vb, kt, sc, dp, st, sr, dka, dva, dks, dvs, dqs, dqr, dqo,
    l_sem, kv_send, kv_recv, in_send, in_recv, st_send, st_recv,
    o_send, o_recv, dq_send, dq_recv, f_send, f_recv,
):
    p = lax.axis_index("pb")
    m = lax.axis_index("mem")
    g, c = m // 2, m % 2
    head = 2 * p + c

    def cols(h):
        return pl.ds(pl.multiple_of(h * DH, DH), DH)

    def local(src, dst, sem):
        pltpu.make_async_copy(src, dst, sem).start()

    def remote(src, dst, send, recv, pb, mem):
        pltpu.make_async_remote_copy(
            src_ref=src, dst_ref=dst, send_sem=send, recv_sem=recv,
            device_id=(pb, mem), device_id_type=MESH,
        ).start()

    def settle(ref, sem):
        pltpu.make_async_copy(ref, ref, sem).wait()

    local(k_hbm.at[:, cols(head)], kb.at[0], l_sem.at[0])
    local(v_hbm.at[:, cols(head)], vb.at[0], l_sem.at[1])
    local(q_hbm.at[:, cols(head)], qb.at[0], in_recv.at[0, 0])
    local(do_hbm.at[:, cols(head)], dob.at[0], in_recv.at[0, 1])

    barrier = pltpu.get_barrier_semaphore()
    for i in range(1, 2 * NB):
        pl.semaphore_signal(barrier, inc=1, device_id=(p ^ (i >> 1), m ^ (i & 1)), device_id_type=MESH)
    for i in range(1, NG):
        pl.semaphore_signal(barrier, inc=1, device_id=(p, m ^ (2 * i)), device_id_type=MESH)
    pl.semaphore_wait(barrier, 2 * NB + NG - 2)

    mate = 2 * p + 1 - c
    remote(k_hbm.at[:, cols(mate)], kb.at[1], kv_send, kv_recv, p, m ^ 1)
    remote(v_hbm.at[:, cols(mate)], vb.at[1], kv_send, kv_recv, p, m ^ 1)
    for i in range(1, NB):
        to = p ^ ORDER[i]
        remote(q_hbm.at[:, cols(2 * to + c)], qb.at[i], in_send.at[0], in_recv.at[i, 0], to, m)
        remote(do_hbm.at[:, cols(2 * to + c)], dob.at[i], in_send.at[1], in_recv.at[i, 1], to, m)

    dka[...] = jnp.zeros_like(dka)
    dva[...] = jnp.zeros_like(dva)
    settle(kb.at[0], l_sem.at[0])
    settle(vb.at[0], l_sem.at[1])
    settle(kb, kv_recv)
    for half in range(2):
        kt[half] = kb[half].T

    def forward(r):
        settle(qb.at[r], in_recv.at[r, 0])
        settle(dob.at[r], in_recv.at[r, 1])
        q = qb[r]
        do = dob[r]
        top = jnp.full((8, RB), -1e30, F32)
        total = jnp.zeros((8, RB), F32)
        term = jnp.zeros((8, RB), F32)
        for half in range(2):
            for j in range(KB // KT):
                rows = pl.ds(j * KT, KT)
                s = lax.dot_general(kb[half, rows, :], q, (((1,), (1,)), ((), ())), preferred_element_type=F32)
                d = lax.dot_general(vb[half, rows, :], do, (((1,), (1,)), ((), ())), preferred_element_type=F32)
                sc[r, half, rows, :] = s
                dp[r, half, rows, :] = d
                s = s.reshape(KT // 8, 8, RB)
                d = d.reshape(KT // 8, 8, RB)
                new = jnp.maximum(top, jnp.max(s, axis=0))
                w = jnp.exp2((top - new) * C2)
                e = jnp.exp2((s - new[None]) * C2)
                total = total * w + jnp.sum(e, axis=0)
                term = term * w + jnp.sum(e * d, axis=0)
                top = new
        peak = jnp.max(top, axis=0, keepdims=True)
        w = jnp.exp2((top - peak) * C2)
        total = jnp.sum(total * w, axis=0, keepdims=True)
        term = jnp.sum(term * w, axis=0, keepdims=True)
        tiles = [v[:, k * 128:k * 128 + 128] for v in (peak, total, term) for k in range(2)]
        st[r] = jnp.concatenate(tiles + [jnp.zeros((2, 128), F32)], axis=0)

    def send_stats(i):
        pair = pl.ds(2 * i, 2)
        local(st.at[pair], sr.at[i, g], st_recv.at[i])
        for n in range(1, NG):
            remote(st.at[pair], sr.at[i, g], st_send, st_recv.at[i], p, m ^ (2 * n))

    def stats(i, k):
        part = sr[i, :, k]
        tm, tl, tt = part[:, 0:2], part[:, 2:4], part[:, 4:6]
        top = jnp.max(tm, axis=0)
        w = jnp.exp2((tm - top) * C2)
        total = jnp.sum(tl * w, axis=0)
        t = jnp.sum(tt * w, axis=0) / total
        b = top * C2 + jnp.log2(total)
        return (jnp.concatenate([v[0:1], v[1:2]], axis=1) for v in (b, t))

    def piece(r, half, rows, b, t):
        pr = jnp.exp2(sc[r, half, rows, :] * C2 - b)
        ds = (pr * (dp[r, half, rows, :] - t)).astype(BF16)
        dv = jnp.dot(pr.astype(BF16), dob[r], preferred_element_type=F32)
        dk = jnp.dot(ds, qb[r], preferred_element_type=F32)
        dq = jnp.dot(kt[half, :, rows], ds, preferred_element_type=F32)
        return dk, dv, dq

    def send_dq(r, dq):
        batch, k = r // BATCH, r % BATCH
        dqs[batch, :, k] = (dq * SCALE).T.astype(BF16).reshape(NG, RB // NG, DH)

        @pl.when(k == BATCH - 1)
        def _():
            local(dqs.at[batch, g], dqr.at[batch, g], dq_recv.at[batch])
            for i in range(1, NG):
                remote(dqs.at[batch, g ^ i], dqr.at[batch, g], dq_send, dq_recv.at[batch], p, m ^ (2 * i))

    def backward(i, k):
        r = 2 * i + k
        b, t = stats(i, k)
        dq = jnp.zeros((DH, RB), F32)
        for half in range(2):
            for j in range(KB // KT):
                rows = pl.ds(j * KT, KT)
                dk, dv, part = piece(r, half, rows, b, t)
                dka[half, rows, :] += dk
                dva[half, rows, :] += dv
                dq += part
        send_dq(r, dq)

    def backward_last():
        r = NB - 1
        b, t = stats(NB // 2 - 1, 1)
        dq = jnp.zeros((DH, RB), F32)
        for e in range(KB // KT):
            for half in range(2):
                j = (p >> 1) ^ (KB // KT - 1 - e)
                rows = pl.ds(pl.multiple_of(j * KT, KT), KT)
                dk, dv, part = piece(r, half, rows, b, t)
                dk = ((dka[half, rows, :] + dk) * SCALE).astype(BF16)
                dv = (dva[half, rows, :] + dv).astype(BF16)
                dq += part
                dks[pl.ds(half * NB + 2 * j, 2)] = dk.reshape(2, KP, DH)
                dvs[pl.ds(half * NB + 2 * j, 2)] = dv.reshape(2, KP, DH)
                for n in range(2):
                    to = p ^ (2 * (KB // KT - 1 - e) + 1 - n)
                    for ref, out, i in ((dks, dk_out, 0), (dvs, dv_out, 1)):
                        if half == 0 and e == KB // KT - 1 and n == 1:
                            local(ref.at[to], out.at[:, cols(head)], o_recv.at[i])
                        else:
                            remote(ref.at[half * NB + to], out.at[:, cols(head)], o_send.at[i], o_recv.at[i], to, m ^ half)
        send_dq(r, dq)

    def lead(i, carry):
        forward(2 * i)
        forward(2 * i + 1)
        send_stats(i)
        return carry

    def steady(i, carry):
        lead(i, carry)
        return rest(i - LAG, carry)

    def rest(i, carry):
        settle(sr.at[i], st_recv.at[i])
        backward(i, 0)
        backward(i, 1)
        return carry

    lax.fori_loop(0, LAG, lead, 0)
    lax.fori_loop(LAG, NB // 2, steady, 0)
    lax.fori_loop(NB // 2 - LAG, NB // 2 - 1, rest, 0)
    settle(sr.at[NB // 2 - 1], st_recv.at[NB // 2 - 1])
    backward(NB // 2 - 1, 0)
    backward_last()

    for batch in range(NB // BATCH):
        settle(dqr.at[batch], dq_recv.at[batch])
        for k in range(BATCH):
            r = batch * BATCH + k
            acc = jnp.sum(dqr[batch, :, k].astype(F32), axis=0)
            dqo[2 * r:2 * r + 2] = acc.reshape(2, 8, DH)
            to = p ^ ORDER[r]
            for e in range(2):
                dst = dq_out.at[:, cols(head)]
                if r == 0 and e == 0:
                    local(dqo.at[c], dst, f_recv)
                else:
                    remote(dqo.at[2 * r + (c ^ e)], dst, f_send, f_recv, to, m ^ e)

    settle(kb, kv_send)
    settle(qb.at[1:], in_send.at[0])
    settle(dob.at[1:], in_send.at[1])
    settle(sr.at[:, 1:], st_send)
    settle(dqs.at[:, 1:], dq_send)
    settle(dqo.at[1:], f_send)
    settle(dks.at[1:], o_send.at[0])
    settle(dvs.at[1:], o_send.at[1])
    settle(dq_out, f_recv)
    settle(dk_out, o_recv.at[0])
    settle(dv_out, o_recv.at[1])


def place(dq, dk, dv, dq_out, dk_out, dv_out, dqv, dkv, dvv, in_sem, out_sem):
    steps = [(dq, dqv, dq_out)]
    for n in range(2):
        rows = pl.ds(n * KP // 2, KP // 2)
        for src, via, dst in ((dk, dkv, dk_out.at[0]), (dv, dvv, dv_out.at[0])):
            steps.append((src.at[rows], via.at[rows], dst.at[rows]))
    fetch = [pltpu.make_async_copy(src, via, in_sem.at[i]) for i, (src, via, _) in enumerate(steps)]
    store = [pltpu.make_async_copy(via, dst, out_sem.at[i]) for i, (_, via, dst) in enumerate(steps)]
    for copy in fetch:
        copy.start()
    for first, second in zip(fetch, store):
        first.wait()
        second.start()
    for copy in store:
        copy.wait()


def shards(queries, keys, values, d_out):
    width = queries.shape[1]
    dma = pltpu.SemaphoreType.DMA
    any_space = pl.BlockSpec(memory_space=pl.ANY)
    dq, dk, dv = pl.pallas_call(
        kernel,
        out_shape=(
            jax.ShapeDtypeStruct((8, width), F32),
            jax.ShapeDtypeStruct((KP, width), BF16),
            jax.ShapeDtypeStruct((KP, width), BF16),
        ),
        in_specs=[any_space] * 4,
        out_specs=[any_space] * 3,
        scratch_shapes=[
            pltpu.VMEM((NB, RB, DH), BF16),
            pltpu.VMEM((NB, RB, DH), BF16),
            pltpu.VMEM((2, KB, DH), BF16),
            pltpu.VMEM((2, KB, DH), BF16),
            pltpu.VMEM((2, DH, KB), BF16),
            pltpu.VMEM((NB, 2, KB, RB), F32),
            pltpu.VMEM((NB, 2, KB, RB), F32),
            pltpu.VMEM((NB, 8, 128), F32),
            pltpu.VMEM((NB // 2, NG, 2, 8, 128), F32),
            pltpu.VMEM((2, KB, DH), F32),
            pltpu.VMEM((2, KB, DH), F32),
            pltpu.VMEM((2 * NB, KP, DH), BF16),
            pltpu.VMEM((2 * NB, KP, DH), BF16),
            pltpu.VMEM((NB // BATCH, NG, BATCH, RB // NG, DH), BF16),
            pltpu.VMEM((NB // BATCH, NG, BATCH, RB // NG, DH), BF16),
            pltpu.VMEM((2 * NB, 8, DH), F32),
            dma((2,)),
            dma,
            dma,
            dma((2,)),
            dma((NB, 2)),
            dma,
            dma((NB // 2,)),
            dma((2,)),
            dma((2,)),
            dma,
            dma((NB // BATCH,)),
            dma,
            dma,
        ],
        compiler_params=pltpu.CompilerParams(
            collective_id=0, has_side_effects=True, vmem_limit_bytes=56 * 2**20
        ),
        cost_estimate=pl.CostEstimate(flops=5 * 2 * 2048 * 2048 * 128, bytes_accessed=12 * 2**20, transcendentals=2 * 2048 * 2048),
    )(queries, keys, values, d_out)
    return pl.pallas_call(
        place,
        out_shape=(
            jax.ShapeDtypeStruct((8, width), F32),
            jax.ShapeDtypeStruct((1, KP, width), BF16),
            jax.ShapeDtypeStruct((1, KP, width), BF16),
        ),
        in_specs=[any_space] * 3,
        out_specs=[any_space] * 3,
        scratch_shapes=[
            pltpu.VMEM((8, width), F32),
            pltpu.VMEM((KP, width), BF16),
            pltpu.VMEM((KP, width), BF16),
            dma((5,)),
            dma((5,)),
        ],
    )(dq, dk, dv)


def solution(mesh):
    return jax.shard_map(
        shards,
        mesh=mesh,
        in_specs=(P("pb", None), P("mem", None), P("mem", None), P("pb", None)),
        out_specs=(P(("pb", "mem"), None), P("mem", "pb", None), P("mem", "pb", None)),
        check_vma=False,
    )
```

```python
import functools
import math

import jax
import jax.numpy as jnp
from jax import lax
from jax.experimental import pallas as pl
from jax.experimental.pallas import tpu as pltpu
from jax.sharding import PartitionSpec as P

MESH = pl.DeviceIdType.MESH
DH = 128
NB = 8
NG = 16
RB = 256
KB = 1024
KP = 128
KT = 256
LAG = 3
BATCH = 2
ORDER = (0, 6, 7, 5, 2, 4, 3, 1)
EARLY = 0
HELD = (0,)
SCALE = DH ** -0.5
C2 = SCALE * math.log2(math.e)
F32 = jnp.float32
BF16 = jnp.bfloat16


def kernel(
    q_hbm, k_hbm, v_hbm, do_hbm, dq_out, dk_out, dv_out,
    qb, dob, kb, vb, kt, sc, dp, st, sr, lp, ld, dka, dva, dks, dvs, dqs, dqr, dqo,
    l_sem, kv_send, kv_recv, in_send, in_recv, st_send, st_recv,
    o_send, o_recv, dq_send, dq_recv, f_send, f_recv,
):
    p = lax.axis_index("pb")
    m = lax.axis_index("mem")
    g, c = m // 2, m % 2
    head = 2 * p + c

    def cols(h):
        return pl.ds(pl.multiple_of(h * DH, DH), DH)

    def local(src, dst, sem):
        pltpu.make_async_copy(src, dst, sem).start()

    def remote(src, dst, send, recv, pb, mem):
        pltpu.make_async_remote_copy(
            src_ref=src, dst_ref=dst, send_sem=send, recv_sem=recv,
            device_id=(pb, mem), device_id_type=MESH,
        ).start()

    def settle(ref, sem):
        pltpu.make_async_copy(ref, ref, sem).wait()

    local(k_hbm.at[:, cols(head)], kb.at[0], l_sem.at[0])
    local(v_hbm.at[:, cols(head)], vb.at[0], l_sem.at[1])
    local(q_hbm.at[:, cols(head)], qb.at[0], in_recv.at[0, 0])
    local(do_hbm.at[:, cols(head)], dob.at[0], in_recv.at[0, 1])

    barrier = pltpu.get_barrier_semaphore()
    for i in range(1, 2 * NB):
        pl.semaphore_signal(barrier, inc=1, device_id=(p ^ (i >> 1), m ^ (i & 1)), device_id_type=MESH)
    for i in range(1, NG):
        pl.semaphore_signal(barrier, inc=1, device_id=(p, m ^ (2 * i)), device_id_type=MESH)
    def score(r, half, state):
        q = qb[r]
        do = dob[r]
        top, total, term = state
        for j in range(KB // KT):
            rows = pl.ds(j * KT, KT)
            s = lax.dot_general(kb[half, rows, :], q, (((1,), (1,)), ((), ())), preferred_element_type=F32)
            d = lax.dot_general(vb[half, rows, :], do, (((1,), (1,)), ((), ())), preferred_element_type=F32)
            sc[r, half, rows, :] = s
            dp[r, half, rows, :] = d
            s = s.reshape(KT // 8, 8, RB)
            d = d.reshape(KT // 8, 8, RB)
            new = jnp.maximum(top, jnp.max(s, axis=0))
            w = jnp.exp2((top - new) * C2)
            e = jnp.exp2((s - new[None]) * C2)
            total = total * w + jnp.sum(e, axis=0)
            term = term * w + jnp.sum(e * d, axis=0)
            top = new
        return top, total, term

    def fresh():
        return jnp.full((8, RB), -1e30, F32), jnp.zeros((8, RB), F32), jnp.zeros((8, RB), F32)

    def settle_in(r):
        settle(qb.at[r], in_recv.at[r, 0])
        settle(dob.at[r], in_recv.at[r, 1])

    def forward(r):
        settle_in(r)
        finish(r, score(r, 1, score(r, 0, fresh())))

    def finish(r, state):
        top, total, term = state
        peak = jnp.max(top, axis=0, keepdims=True)
        w = jnp.exp2((top - peak) * C2)
        total = jnp.sum(total * w, axis=0, keepdims=True)
        term = jnp.sum(term * w, axis=0, keepdims=True)
        tiles = [v[:, k * 128:k * 128 + 128] for v in (peak, total, term) for k in range(2)]
        st[r] = jnp.concatenate(tiles + [jnp.zeros((2, 128), F32)], axis=0)

    def send_stats(i):
        pair = pl.ds(2 * i, 2)
        local(st.at[pair], sr.at[i, g], st_recv.at[i])
        for n in range(1, NG):
            remote(st.at[pair], sr.at[i, g], st_send, st_recv.at[i], p, m ^ (2 * n))

    def stats(i, k):
        part = sr[i, :, k]
        tm, tl, tt = part[:, 0:2], part[:, 2:4], part[:, 4:6]
        top = jnp.max(tm, axis=0)
        w = jnp.exp2((tm - top) * C2)
        total = jnp.sum(tl * w, axis=0)
        t = jnp.sum(tt * w, axis=0) / total
        b = top * C2 + jnp.log2(total)
        return (jnp.concatenate([v[0:1], v[1:2]], axis=1) for v in (b, t))

    def weigh(r, half, rows, b, t):
        pr = jnp.exp2(sc[r, half, rows, :] * C2 - b)
        ds = (pr * (dp[r, half, rows, :] - t)).astype(BF16)
        return pr.astype(BF16), ds

    def piece(r, half, rows, b, t):
        pr, ds = weigh(r, half, rows, b, t)
        dv = jnp.dot(pr, dob[r], preferred_element_type=F32)
        dk = jnp.dot(ds, qb[r], preferred_element_type=F32)
        dq = jnp.dot(kt[half, :, rows], ds, preferred_element_type=F32)
        return dk, dv, dq

    def send_dq(r, dq):
        batch, k = r // BATCH, r % BATCH
        dqs[batch, :, k] = (dq * SCALE).T.astype(BF16).reshape(NG, RB // NG, DH)

        @pl.when(k == BATCH - 1)
        def _():
            local(dqs.at[batch, g], dqr.at[batch, g], dq_recv.at[batch])
            for i in range(1, NG):
                remote(dqs.at[batch, g ^ i], dqr.at[batch, g], dq_send, dq_recv.at[batch], p, m ^ (2 * i))

    def backward(i, k):
        r = 2 * i + k
        b, t = stats(i, k)
        dq = jnp.zeros((DH, RB), F32)
        for half in range(2):
            for j in range(KB // KT):
                rows = pl.ds(j * KT, KT)
                dk, dv, part = piece(r, half, rows, b, t)
                dka[half, rows, :] += dk
                dva[half, rows, :] += dv
                dq += part
        send_dq(r, dq)

    def finals(batch):
        settle(dqr.at[batch], dq_recv.at[batch])
        for k in range(BATCH):
            r = batch * BATCH + k
            acc = jnp.sum(dqr[batch, :, k].astype(F32), axis=0)
            dqo[2 * r:2 * r + 2] = acc.reshape(2, 8, DH)
            to = p ^ ORDER[r]
            for e in range(2):
                dst = dq_out.at[:, cols(head)]
                if r == 0 and e == 0:
                    local(dqo.at[c], dst, f_recv)
                else:
                    remote(dqo.at[2 * r + (c ^ e)], dst, f_send, f_recv, to, m ^ e)

    def ship(half, step):
        to = p ^ step
        for ref, out, i in ((dks, dk_out, 0), (dvs, dv_out, 1)):
            if half == 0 and step == 0:
                local(ref.at[to], out.at[:, cols(head)], o_recv.at[i])
            else:
                remote(ref.at[half * NB + to], out.at[:, cols(head)], o_send.at[i], o_recv.at[i], to, m ^ half)

    def backward_last():
        pair = NB // 2 - 1
        for k in range(2):
            r = 2 * pair + k
            b, t = stats(pair, k)
            dq = jnp.zeros((DH, RB), F32)
            for half in range(2):
                for j in range(KB // KT):
                    rows = pl.ds(j * KT, KT)
                    pr, ds = weigh(r, half, rows, b, t)
                    lp[half, rows, k * RB:(k + 1) * RB] = pr
                    ld[half, rows, k * RB:(k + 1) * RB] = ds
                    dq += jnp.dot(kt[half, :, rows], ds, preferred_element_type=F32)
            send_dq(r, dq)
        q = qb[2 * pair:2 * pair + 2].reshape(2 * RB, DH)
        do = dob[2 * pair:2 * pair + 2].reshape(2 * RB, DH)
        for e in reversed(range(KB // KT)):
            for half in range(2):
                j = (p >> 1) ^ e
                rows = pl.ds(pl.multiple_of(j * KT, KT), KT)
                dk = dka[half, rows, :] + jnp.dot(ld[half, rows, :], q, preferred_element_type=F32)
                dv = dva[half, rows, :] + jnp.dot(lp[half, rows, :], do, preferred_element_type=F32)
                dks[pl.ds(half * NB + 2 * j, 2)] = (dk * SCALE).astype(BF16).reshape(2, KP, DH)
                dvs[pl.ds(half * NB + 2 * j, 2)] = dv.astype(BF16).reshape(2, KP, DH)
                for step in (2 * e + 1, 2 * e):
                    if step not in HELD:
                        ship(half, step)

    def lead(i, carry):
        forward(2 * i)
        forward(2 * i + 1)
        send_stats(i)
        return carry

    def steady(i, carry):
        lead(i, carry)
        return rest(i - LAG, carry)

    def rest(i, carry):
        settle(sr.at[i], st_recv.at[i])
        backward(i, 0)
        backward(i, 1)
        return carry

    dka[...] = jnp.zeros_like(dka)
    dva[...] = jnp.zeros_like(dva)
    settle(kb.at[0], l_sem.at[0])
    settle(vb.at[0], l_sem.at[1])
    settle_in(0)
    state = score(0, 0, fresh())
    pl.semaphore_wait(barrier, 2 * NB + NG - 2)

    mate = 2 * p + 1 - c
    remote(k_hbm.at[:, cols(mate)], kb.at[1], kv_send, kv_recv, p, m ^ 1)
    remote(v_hbm.at[:, cols(mate)], vb.at[1], kv_send, kv_recv, p, m ^ 1)
    for i in range(1, NB):
        to = p ^ ORDER[i]
        remote(q_hbm.at[:, cols(2 * to + c)], qb.at[i], in_send.at[0], in_recv.at[i, 0], to, m)
        remote(do_hbm.at[:, cols(2 * to + c)], dob.at[i], in_send.at[1], in_recv.at[i, 1], to, m)

    kt[0] = kb[0].T
    settle(kb, kv_recv)
    finish(0, score(0, 1, state))
    forward(1)
    send_stats(0)
    kt[1] = kb[1].T
    lax.fori_loop(1, LAG, lead, 0)
    lax.fori_loop(LAG, NB // 2, steady, 0)
    lax.fori_loop(NB // 2 - LAG, NB // 2 - 1, rest, 0)
    for batch in range(EARLY):
        finals(batch)
    settle(sr.at[NB // 2 - 1], st_recv.at[NB // 2 - 1])
    backward_last()
    for batch in range(EARLY, NB // BATCH):
        finals(batch)
    for step in HELD:
        for half in (1, 0):
            ship(half, step)

    settle(kb, kv_send)
    settle(qb.at[1:], in_send.at[0])
    settle(dob.at[1:], in_send.at[1])
    settle(sr.at[:, 1:], st_send)
    settle(dqs.at[:, 1:], dq_send)
    settle(dqo.at[1:], f_send)
    settle(dks.at[1:], o_send.at[0])
    settle(dvs.at[1:], o_send.at[1])
    settle(dq_out, f_recv)
    settle(dk_out, o_recv.at[0])
    settle(dv_out, o_recv.at[1])


def place(dq, dk, dv, dq_out, dk_out, dv_out, dqv, dkv, dvv, in_sem, out_sem):
    steps = [(dq, dqv, dq_out)]
    for n in range(2):
        rows = pl.ds(n * KP // 2, KP // 2)
        for src, via, dst in ((dk, dkv, dk_out.at[0]), (dv, dvv, dv_out.at[0])):
            steps.append((src.at[rows], via.at[rows], dst.at[rows]))
    fetch = [pltpu.make_async_copy(src, via, in_sem.at[i]) for i, (src, via, _) in enumerate(steps)]
    store = [pltpu.make_async_copy(via, dst, out_sem.at[i]) for i, (_, via, dst) in enumerate(steps)]
    for copy in fetch:
        copy.start()
    for first, second in zip(fetch, store):
        first.wait()
        second.start()
    for copy in store:
        copy.wait()


def shards(queries, keys, values, d_out):
    width = queries.shape[1]
    dma = pltpu.SemaphoreType.DMA
    any_space = pl.BlockSpec(memory_space=pl.ANY)
    dq, dk, dv = pl.pallas_call(
        kernel,
        out_shape=(
            jax.ShapeDtypeStruct((8, width), F32),
            jax.ShapeDtypeStruct((KP, width), BF16),
            jax.ShapeDtypeStruct((KP, width), BF16),
        ),
        in_specs=[any_space] * 4,
        out_specs=[any_space] * 3,
        scratch_shapes=[
            pltpu.VMEM((NB, RB, DH), BF16),
            pltpu.VMEM((NB, RB, DH), BF16),
            pltpu.VMEM((2, KB, DH), BF16),
            pltpu.VMEM((2, KB, DH), BF16),
            pltpu.VMEM((2, DH, KB), BF16),
            pltpu.VMEM((NB, 2, KB, RB), F32),
            pltpu.VMEM((NB, 2, KB, RB), F32),
            pltpu.VMEM((NB, 8, 128), F32),
            pltpu.VMEM((NB // 2, NG, 2, 8, 128), F32),
            pltpu.VMEM((2, KB, 2 * RB), BF16),
            pltpu.VMEM((2, KB, 2 * RB), BF16),
            pltpu.VMEM((2, KB, DH), F32),
            pltpu.VMEM((2, KB, DH), F32),
            pltpu.VMEM((2 * NB, KP, DH), BF16),
            pltpu.VMEM((2 * NB, KP, DH), BF16),
            pltpu.VMEM((NB // BATCH, NG, BATCH, RB // NG, DH), BF16),
            pltpu.VMEM((NB // BATCH, NG, BATCH, RB // NG, DH), BF16),
            pltpu.VMEM((2 * NB, 8, DH), F32),
            dma((2,)),
            dma,
            dma,
            dma((2,)),
            dma((NB, 2)),
            dma,
            dma((NB // 2,)),
            dma((2,)),
            dma((2,)),
            dma,
            dma((NB // BATCH,)),
            dma,
            dma,
        ],
        compiler_params=pltpu.CompilerParams(
            collective_id=0, has_side_effects=True, vmem_limit_bytes=56 * 2**20
        ),
        cost_estimate=pl.CostEstimate(flops=5 * 2 * 2048 * 2048 * 128, bytes_accessed=12 * 2**20, transcendentals=2 * 2048 * 2048),
    )(queries, keys, values, d_out)
    return pl.pallas_call(
        place,
        out_shape=(
            jax.ShapeDtypeStruct((8, width), F32),
            jax.ShapeDtypeStruct((1, KP, width), BF16),
            jax.ShapeDtypeStruct((1, KP, width), BF16),
        ),
        in_specs=[any_space] * 3,
        out_specs=[any_space] * 3,
        scratch_shapes=[
            pltpu.VMEM((8, width), F32),
            pltpu.VMEM((KP, width), BF16),
            pltpu.VMEM((KP, width), BF16),
            dma((5,)),
            dma((5,)),
        ],
    )(dq, dk, dv)


def solution(mesh):
    return jax.shard_map(
        shards,
        mesh=mesh,
        in_specs=(P("pb", None), P("mem", None), P("mem", None), P("pb", None)),
        out_specs=(P(("pb", "mem"), None), P("mem", "pb", None), P("mem", "pb", None)),
        check_vma=False,
    )
```

```python
import functools
import math

import jax
import jax.numpy as jnp
from jax import lax
from jax.experimental import pallas as pl
from jax.experimental.pallas import tpu as pltpu
from jax.sharding import PartitionSpec as P

MESH = pl.DeviceIdType.MESH
DH = 128
NB = 8
NG = 16
RB = 256
KB = 1024
KP = 128
KT = 256
LAG = 3
BATCH = 2
ORDER = (0, 6, 7, 5, 2, 4, 3, 1)
EARLY = 0
HELD = (0,)
SCALE = DH ** -0.5
C2 = SCALE * math.log2(math.e)
F32 = jnp.float32
BF16 = jnp.bfloat16


def kernel(
    q_hbm, k_hbm, v_hbm, do_hbm, dq_out, dk_out, dv_out,
    qb, dob, kb, vb, kt, sc, dp, st, sr, lp, ld, dka, dva, dks, dvs, dqs, dqr, dqo,
    l_sem, kv_send, kv_recv, in_send, in_recv, st_send, st_recv,
    o_send, o_recv, dq_send, dq_recv, f_send, f_recv,
):
    p = lax.axis_index("pb")
    m = lax.axis_index("mem")
    g, c = m // 2, m % 2
    head = 2 * p + c

    def cols(h):
        return pl.ds(pl.multiple_of(h * DH, DH), DH)

    def local(src, dst, sem):
        pltpu.make_async_copy(src, dst, sem).start()

    def remote(src, dst, send, recv, pb, mem):
        pltpu.make_async_remote_copy(
            src_ref=src, dst_ref=dst, send_sem=send, recv_sem=recv,
            device_id=(pb, mem), device_id_type=MESH,
        ).start()

    def others():
        for ahead in (4, 3, 5, 2, 6, 1, 7, 0):
            for flip in (0, NG):
                if ahead or flip:
                    yield (m // NG * NG + flip) % (2 * NG) + (m + 2 * ahead) % NG

    def settle(ref, sem):
        pltpu.make_async_copy(ref, ref, sem).wait()

    local(k_hbm.at[:, cols(head)], kb.at[0], l_sem.at[0])
    local(v_hbm.at[:, cols(head)], vb.at[0], l_sem.at[1])
    local(q_hbm.at[:, cols(head)], qb.at[0], in_recv.at[0, 0])
    local(do_hbm.at[:, cols(head)], dob.at[0], in_recv.at[0, 1])

    barrier = pltpu.get_barrier_semaphore()
    for i in range(1, 2 * NB):
        pl.semaphore_signal(barrier, inc=1, device_id=(p ^ (i >> 1), m ^ (i & 1)), device_id_type=MESH)
    for i in range(1, NG):
        pl.semaphore_signal(barrier, inc=1, device_id=(p, m ^ (2 * i)), device_id_type=MESH)
    def score(r, half, state):
        q = qb[r]
        do = dob[r]
        top, total, term = state
        for j in range(KB // KT):
            rows = pl.ds(j * KT, KT)
            s = lax.dot_general(kb[half, rows, :], q, (((1,), (1,)), ((), ())), preferred_element_type=F32)
            d = lax.dot_general(vb[half, rows, :], do, (((1,), (1,)), ((), ())), preferred_element_type=F32)
            sc[r, half, rows, :] = s
            dp[r, half, rows, :] = d
            s = s.reshape(KT // 8, 8, RB)
            d = d.reshape(KT // 8, 8, RB)
            new = jnp.maximum(top, jnp.max(s, axis=0))
            w = jnp.exp2((top - new) * C2)
            e = jnp.exp2((s - new[None]) * C2)
            total = total * w + jnp.sum(e, axis=0)
            term = term * w + jnp.sum(e * d, axis=0)
            top = new
        return top, total, term

    def fresh():
        return jnp.full((8, RB), -1e30, F32), jnp.zeros((8, RB), F32), jnp.zeros((8, RB), F32)

    def settle_in(r):
        settle(qb.at[r], in_recv.at[r, 0])
        settle(dob.at[r], in_recv.at[r, 1])

    def forward(r):
        settle_in(r)
        finish(r, score(r, 1, score(r, 0, fresh())))

    def finish(r, state):
        top, total, term = state
        peak = jnp.max(top, axis=0, keepdims=True)
        w = jnp.exp2((top - peak) * C2)
        total = jnp.sum(total * w, axis=0, keepdims=True)
        term = jnp.sum(term * w, axis=0, keepdims=True)
        tiles = [v[:, k * 128:k * 128 + 128] for v in (peak, total, term) for k in range(2)]
        st[r] = jnp.concatenate(tiles + [jnp.zeros((2, 128), F32)], axis=0)

    def send_stats(i):
        pair = pl.ds(2 * i, 2)
        local(st.at[pair], sr.at[i, g], st_recv.at[i])
        for to in others():
            remote(st.at[pair], sr.at[i, g], st_send, st_recv.at[i], p, to)

    def stats(i, k):
        part = sr[i, :, k]
        tm, tl, tt = part[:, 0:2], part[:, 2:4], part[:, 4:6]
        top = jnp.max(tm, axis=0)
        w = jnp.exp2((tm - top) * C2)
        total = jnp.sum(tl * w, axis=0)
        t = jnp.sum(tt * w, axis=0) / total
        b = top * C2 + jnp.log2(total)
        return (jnp.concatenate([v[0:1], v[1:2]], axis=1) for v in (b, t))

    def weigh(r, half, rows, b, t):
        pr = jnp.exp2(sc[r, half, rows, :] * C2 - b)
        ds = (pr * (dp[r, half, rows, :] - t)).astype(BF16)
        return pr.astype(BF16), ds

    def piece(r, half, rows, b, t):
        pr, ds = weigh(r, half, rows, b, t)
        dv = jnp.dot(pr, dob[r], preferred_element_type=F32)
        dk = jnp.dot(ds, qb[r], preferred_element_type=F32)
        dq = jnp.dot(kt[half, :, rows], ds, preferred_element_type=F32)
        return dk, dv, dq

    def send_dq(r, dq):
        batch, k = r // BATCH, r % BATCH
        dqs[batch, :, k] = (dq * SCALE).T.astype(BF16).reshape(NG, RB // NG, DH)

        @pl.when(k == BATCH - 1)
        def _():
            local(dqs.at[batch, g], dqr.at[batch, g], dq_recv.at[batch])
            for to in others():
                remote(dqs.at[batch, to // 2], dqr.at[batch, g], dq_send, dq_recv.at[batch], p, to)

    def backward(i, k):
        r = 2 * i + k
        b, t = stats(i, k)
        dq = jnp.zeros((DH, RB), F32)
        for half in range(2):
            for j in range(KB // KT):
                rows = pl.ds(j * KT, KT)
                dk, dv, part = piece(r, half, rows, b, t)
                dka[half, rows, :] += dk
                dva[half, rows, :] += dv
                dq += part
        send_dq(r, dq)

    def finals(batch):
        settle(dqr.at[batch], dq_recv.at[batch])
        for k in range(BATCH):
            r = batch * BATCH + k
            acc = jnp.sum(dqr[batch, :, k].astype(F32), axis=0)
            dqo[2 * r:2 * r + 2] = acc.reshape(2, 8, DH)
            to = p ^ ORDER[r]
            for e in range(2):
                dst = dq_out.at[:, cols(head)]
                if r == 0 and e == 0:
                    local(dqo.at[c], dst, f_recv)
                else:
                    remote(dqo.at[2 * r + (c ^ e)], dst, f_send, f_recv, to, m ^ e)

    def ship(half, step):
        to = p ^ step
        for ref, out, i in ((dks, dk_out, 0), (dvs, dv_out, 1)):
            if half == 0 and step == 0:
                local(ref.at[to], out.at[:, cols(head)], o_recv.at[i])
            else:
                remote(ref.at[half * NB + to], out.at[:, cols(head)], o_send.at[i], o_recv.at[i], to, m ^ half)

    def backward_last():
        pair = NB // 2 - 1
        for k in range(2):
            r = 2 * pair + k
            b, t = stats(pair, k)
            dq = jnp.zeros((DH, RB), F32)
            for half in range(2):
                for j in range(KB // KT):
                    rows = pl.ds(j * KT, KT)
                    pr, ds = weigh(r, half, rows, b, t)
                    lp[half, rows, k * RB:(k + 1) * RB] = pr
                    ld[half, rows, k * RB:(k + 1) * RB] = ds
                    dq += jnp.dot(kt[half, :, rows], ds, preferred_element_type=F32)
            send_dq(r, dq)
        q = qb[2 * pair:2 * pair + 2].reshape(2 * RB, DH)
        do = dob[2 * pair:2 * pair + 2].reshape(2 * RB, DH)
        for e in reversed(range(KB // KT)):
            for half in range(2):
                j = (p >> 1) ^ e
                rows = pl.ds(pl.multiple_of(j * KT, KT), KT)
                dk = dka[half, rows, :] + jnp.dot(ld[half, rows, :], q, preferred_element_type=F32)
                dv = dva[half, rows, :] + jnp.dot(lp[half, rows, :], do, preferred_element_type=F32)
                dks[pl.ds(half * NB + 2 * j, 2)] = (dk * SCALE).astype(BF16).reshape(2, KP, DH)
                dvs[pl.ds(half * NB + 2 * j, 2)] = dv.astype(BF16).reshape(2, KP, DH)
                for step in (2 * e + 1, 2 * e):
                    if step not in HELD:
                        ship(half, step)

    def lead(i, carry):
        forward(2 * i)
        forward(2 * i + 1)
        send_stats(i)
        return carry

    def steady(i, carry):
        lead(i, carry)
        return rest(i - LAG, carry)

    def rest(i, carry):
        settle(sr.at[i], st_recv.at[i])
        backward(i, 0)
        backward(i, 1)
        return carry

    dka[...] = jnp.zeros_like(dka)
    dva[...] = jnp.zeros_like(dva)
    settle(kb.at[0], l_sem.at[0])
    settle(vb.at[0], l_sem.at[1])
    settle_in(0)
    state = score(0, 0, fresh())
    pl.semaphore_wait(barrier, 2 * NB + NG - 2)

    mate = 2 * p + 1 - c
    remote(k_hbm.at[:, cols(mate)], kb.at[1], kv_send, kv_recv, p, m ^ 1)
    remote(v_hbm.at[:, cols(mate)], vb.at[1], kv_send, kv_recv, p, m ^ 1)
    for i in range(1, NB):
        to = p ^ ORDER[i]
        remote(q_hbm.at[:, cols(2 * to + c)], qb.at[i], in_send.at[0], in_recv.at[i, 0], to, m)
        remote(do_hbm.at[:, cols(2 * to + c)], dob.at[i], in_send.at[1], in_recv.at[i, 1], to, m)

    kt[0] = kb[0].T
    settle(kb, kv_recv)
    finish(0, score(0, 1, state))
    forward(1)
    send_stats(0)
    kt[1] = kb[1].T
    lax.fori_loop(1, LAG, lead, 0)
    lax.fori_loop(LAG, NB // 2, steady, 0)
    lax.fori_loop(NB // 2 - LAG, NB // 2 - 1, rest, 0)
    for batch in range(EARLY):
        finals(batch)
    settle(sr.at[NB // 2 - 1], st_recv.at[NB // 2 - 1])
    backward_last()
    for batch in range(EARLY, NB // BATCH):
        finals(batch)
    for step in HELD:
        for half in (1, 0):
            ship(half, step)

    settle(kb, kv_send)
    settle(qb.at[1:], in_send.at[0])
    settle(dob.at[1:], in_send.at[1])
    settle(sr.at[:, 1:], st_send)
    settle(dqs.at[:, 1:], dq_send)
    settle(dqo.at[1:], f_send)
    settle(dks.at[1:], o_send.at[0])
    settle(dvs.at[1:], o_send.at[1])
    settle(dq_out, f_recv)
    settle(dk_out, o_recv.at[0])
    settle(dv_out, o_recv.at[1])


def place(dq, dk, dv, dq_out, dk_out, dv_out, dqv, dkv, dvv, in_sem, out_sem):
    steps = [(dq, dqv, dq_out)]
    for n in range(2):
        rows = pl.ds(n * KP // 2, KP // 2)
        for src, via, dst in ((dk, dkv, dk_out.at[0]), (dv, dvv, dv_out.at[0])):
            steps.append((src.at[rows], via.at[rows], dst.at[rows]))
    fetch = [pltpu.make_async_copy(src, via, in_sem.at[i]) for i, (src, via, _) in enumerate(steps)]
    store = [pltpu.make_async_copy(via, dst, out_sem.at[i]) for i, (_, via, dst) in enumerate(steps)]
    for copy in fetch:
        copy.start()
    for first, second in zip(fetch, store):
        first.wait()
        second.start()
    for copy in store:
        copy.wait()


def shards(queries, keys, values, d_out):
    width = queries.shape[1]
    dma = pltpu.SemaphoreType.DMA
    any_space = pl.BlockSpec(memory_space=pl.ANY)
    dq, dk, dv = pl.pallas_call(
        kernel,
        out_shape=(
            jax.ShapeDtypeStruct((8, width), F32),
            jax.ShapeDtypeStruct((KP, width), BF16),
            jax.ShapeDtypeStruct((KP, width), BF16),
        ),
        in_specs=[any_space] * 4,
        out_specs=[any_space] * 3,
        scratch_shapes=[
            pltpu.VMEM((NB, RB, DH), BF16),
            pltpu.VMEM((NB, RB, DH), BF16),
            pltpu.VMEM((2, KB, DH), BF16),
            pltpu.VMEM((2, KB, DH), BF16),
            pltpu.VMEM((2, DH, KB), BF16),
            pltpu.VMEM((NB, 2, KB, RB), F32),
            pltpu.VMEM((NB, 2, KB, RB), F32),
            pltpu.VMEM((NB, 8, 128), F32),
            pltpu.VMEM((NB // 2, NG, 2, 8, 128), F32),
            pltpu.VMEM((2, KB, 2 * RB), BF16),
            pltpu.VMEM((2, KB, 2 * RB), BF16),
            pltpu.VMEM((2, KB, DH), F32),
            pltpu.VMEM((2, KB, DH), F32),
            pltpu.VMEM((2 * NB, KP, DH), BF16),
            pltpu.VMEM((2 * NB, KP, DH), BF16),
            pltpu.VMEM((NB // BATCH, NG, BATCH, RB // NG, DH), BF16),
            pltpu.VMEM((NB // BATCH, NG, BATCH, RB // NG, DH), BF16),
            pltpu.VMEM((2 * NB, 8, DH), F32),
            dma((2,)),
            dma,
            dma,
            dma((2,)),
            dma((NB, 2)),
            dma,
            dma((NB // 2,)),
            dma((2,)),
            dma((2,)),
            dma,
            dma((NB // BATCH,)),
            dma,
            dma,
        ],
        compiler_params=pltpu.CompilerParams(
            collective_id=0, has_side_effects=True, vmem_limit_bytes=56 * 2**20
        ),
        cost_estimate=pl.CostEstimate(flops=5 * 2 * 2048 * 2048 * 128, bytes_accessed=12 * 2**20, transcendentals=2 * 2048 * 2048),
    )(queries, keys, values, d_out)
    return pl.pallas_call(
        place,
        out_shape=(
            jax.ShapeDtypeStruct((8, width), F32),
            jax.ShapeDtypeStruct((1, KP, width), BF16),
            jax.ShapeDtypeStruct((1, KP, width), BF16),
        ),
        in_specs=[any_space] * 3,
        out_specs=[any_space] * 3,
        scratch_shapes=[
            pltpu.VMEM((8, width), F32),
            pltpu.VMEM((KP, width), BF16),
            pltpu.VMEM((KP, width), BF16),
            dma((5,)),
            dma((5,)),
        ],
    )(dq, dk, dv)


def solution(mesh):
    return jax.shard_map(
        shards,
        mesh=mesh,
        in_specs=(P("pb", None), P("mem", None), P("mem", None), P("pb", None)),
        out_specs=(P(("pb", "mem"), None), P("mem", "pb", None), P("mem", "pb", None)),
        check_vma=False,
    )
```

```python
import functools
import math

import jax
import jax.numpy as jnp
from jax import lax
from jax.experimental import pallas as pl
from jax.experimental.pallas import tpu as pltpu
from jax.sharding import PartitionSpec as P

MESH = pl.DeviceIdType.MESH
DH = 128
NB = 8
NG = 16
RB = 256
KB = 1024
KP = 128
KT = 256
LAG = 3
BATCH = 2
ORDER = (0, 6, 7, 5, 2, 4, 3, 1)
EARLY = 1
HELD = (0,)
SCALE = DH ** -0.5
C2 = SCALE * math.log2(math.e)
F32 = jnp.float32
BF16 = jnp.bfloat16


def kernel(
    q_hbm, k_hbm, v_hbm, do_hbm, dq_out, dk_out, dv_out,
    qb, dob, kb, vb, kt, sc, dp, st, sr, lp, ld, dka, dva, dks, dvs, dqs, dqr, dqo,
    l_sem, kv_send, kv_recv, in_send, in_recv, st_send, st_recv,
    o_send, o_recv, dq_send, dq_recv, f_send, f_recv,
):
    p = lax.axis_index("pb")
    m = lax.axis_index("mem")
    g, c = m // 2, m % 2
    head = 2 * p + c

    def cols(h):
        return pl.ds(pl.multiple_of(h * DH, DH), DH)

    def local(src, dst, sem):
        pltpu.make_async_copy(src, dst, sem).start()

    def remote(src, dst, send, recv, pb, mem):
        pltpu.make_async_remote_copy(
            src_ref=src, dst_ref=dst, send_sem=send, recv_sem=recv,
            device_id=(pb, mem), device_id_type=MESH,
        ).start()

    def others():
        for ahead in (4, 3, 5, 2, 6, 1, 7, 0):
            for flip in (0, NG):
                if ahead or flip:
                    yield (m // NG * NG + flip) % (2 * NG) + (m + 2 * ahead) % NG

    def settle(ref, sem):
        pltpu.make_async_copy(ref, ref, sem).wait()

    local(k_hbm.at[:, cols(head)], kb.at[0], l_sem.at[0])
    local(v_hbm.at[:, cols(head)], vb.at[0], l_sem.at[1])
    local(q_hbm.at[:, cols(head)], qb.at[0], in_recv.at[0, 0])
    local(do_hbm.at[:, cols(head)], dob.at[0], in_recv.at[0, 1])

    barrier = pltpu.get_barrier_semaphore()
    for i in range(1, 2 * NB):
        pl.semaphore_signal(barrier, inc=1, device_id=(p ^ (i >> 1), m ^ (i & 1)), device_id_type=MESH)
    for i in range(1, NG):
        pl.semaphore_signal(barrier, inc=1, device_id=(p, m ^ (2 * i)), device_id_type=MESH)
    def score(r, half, state):
        q = qb[r]
        do = dob[r]
        top, total, term = state
        for j in range(KB // KT):
            rows = pl.ds(j * KT, KT)
            s = lax.dot_general(kb[half, rows, :], q, (((1,), (1,)), ((), ())), preferred_element_type=F32)
            d = lax.dot_general(vb[half, rows, :], do, (((1,), (1,)), ((), ())), preferred_element_type=F32)
            sc[r, half, rows, :] = s
            dp[r, half, rows, :] = d
            s = s.reshape(KT // 8, 8, RB)
            d = d.reshape(KT // 8, 8, RB)
            new = jnp.maximum(top, jnp.max(s, axis=0))
            w = jnp.exp2((top - new) * C2)
            e = jnp.exp2((s - new[None]) * C2)
            total = total * w + jnp.sum(e, axis=0)
            term = term * w + jnp.sum(e * d, axis=0)
            top = new
        return top, total, term

    def fresh():
        return jnp.full((8, RB), -1e30, F32), jnp.zeros((8, RB), F32), jnp.zeros((8, RB), F32)

    def settle_in(r):
        settle(qb.at[r], in_recv.at[r, 0])
        settle(dob.at[r], in_recv.at[r, 1])

    def forward(r):
        settle_in(r)
        finish(r, score(r, 1, score(r, 0, fresh())))

    def finish(r, state):
        top, total, term = state
        peak = jnp.max(top, axis=0, keepdims=True)
        w = jnp.exp2((top - peak) * C2)
        total = jnp.sum(total * w, axis=0, keepdims=True)
        term = jnp.sum(term * w, axis=0, keepdims=True)
        tiles = [v[:, k * 128:k * 128 + 128] for v in (peak, total, term) for k in range(2)]
        st[r] = jnp.concatenate(tiles + [jnp.zeros((2, 128), F32)], axis=0)

    def send_stats(i):
        pair = pl.ds(2 * i, 2)
        local(st.at[pair], sr.at[i, g], st_recv.at[i])
        for to in others():
            remote(st.at[pair], sr.at[i, g], st_send, st_recv.at[i], p, to)

    def stats(i, k):
        part = sr[i, :, k]
        tm, tl, tt = part[:, 0:2], part[:, 2:4], part[:, 4:6]
        top = jnp.max(tm, axis=0)
        w = jnp.exp2((tm - top) * C2)
        total = jnp.sum(tl * w, axis=0)
        t = jnp.sum(tt * w, axis=0) / total
        b = top * C2 + jnp.log2(total)
        return (jnp.concatenate([v[0:1], v[1:2]], axis=1) for v in (b, t))

    def weigh(r, half, rows, b, t):
        pr = jnp.exp2(sc[r, half, rows, :] * C2 - b)
        ds = (pr * (dp[r, half, rows, :] - t)).astype(BF16)
        return pr.astype(BF16), ds

    def piece(r, half, rows, b, t):
        pr, ds = weigh(r, half, rows, b, t)
        dv = jnp.dot(pr, dob[r], preferred_element_type=F32)
        dk = jnp.dot(ds, qb[r], preferred_element_type=F32)
        dq = jnp.dot(kt[half, :, rows], ds, preferred_element_type=F32)
        return dk, dv, dq

    def send_dq(r, dq):
        batch, k = r // BATCH, r % BATCH
        dqs[batch, :, k] = (dq * SCALE).T.astype(BF16).reshape(NG, RB // NG, DH)

        @pl.when(k == BATCH - 1)
        def _():
            local(dqs.at[batch, g], dqr.at[batch, g], dq_recv.at[batch])
            for to in others():
                remote(dqs.at[batch, to // 2], dqr.at[batch, g], dq_send, dq_recv.at[batch], p, to)

    def backward(i, k):
        r = 2 * i + k
        b, t = stats(i, k)
        dq = jnp.zeros((DH, RB), F32)
        for half in range(2):
            for j in range(KB // KT):
                rows = pl.ds(j * KT, KT)
                dk, dv, part = piece(r, half, rows, b, t)
                dka[half, rows, :] += dk
                dva[half, rows, :] += dv
                dq += part
        send_dq(r, dq)

    def finals(batch):
        settle(dqr.at[batch], dq_recv.at[batch])
        for k in range(BATCH):
            r = batch * BATCH + k
            acc = jnp.sum(dqr[batch, :, k].astype(F32), axis=0)
            dqo[2 * r:2 * r + 2] = acc.reshape(2, 8, DH)
            to = p ^ ORDER[r]
            for e in range(2):
                dst = dq_out.at[:, cols(head)]
                if r == 0 and e == 0:
                    local(dqo.at[c], dst, f_recv)
                else:
                    remote(dqo.at[2 * r + (c ^ e)], dst, f_send, f_recv, to, m ^ e)

    def ship(half, step):
        to = p ^ step
        for ref, out, i in ((dks, dk_out, 0), (dvs, dv_out, 1)):
            if half == 0 and step == 0:
                local(ref.at[to], out.at[:, cols(head)], o_recv.at[i])
            else:
                remote(ref.at[half * NB + to], out.at[:, cols(head)], o_send.at[i], o_recv.at[i], to, m ^ half)

    def backward_last():
        pair = NB // 2 - 1
        for k in range(2):
            r = 2 * pair + k
            b, t = stats(pair, k)
            dq = jnp.zeros((DH, RB), F32)
            for half in range(2):
                for j in range(KB // KT):
                    rows = pl.ds(j * KT, KT)
                    pr, ds = weigh(r, half, rows, b, t)
                    lp[half, rows, k * RB:(k + 1) * RB] = pr
                    ld[half, rows, k * RB:(k + 1) * RB] = ds
                    dq += jnp.dot(kt[half, :, rows], ds, preferred_element_type=F32)
            send_dq(r, dq)
        q = qb[2 * pair:2 * pair + 2].reshape(2 * RB, DH)
        do = dob[2 * pair:2 * pair + 2].reshape(2 * RB, DH)
        for e in reversed(range(KB // KT)):
            for half in range(2):
                j = (p >> 1) ^ e
                rows = pl.ds(pl.multiple_of(j * KT, KT), KT)
                dk = dka[half, rows, :] + jnp.dot(ld[half, rows, :], q, preferred_element_type=F32)
                dv = dva[half, rows, :] + jnp.dot(lp[half, rows, :], do, preferred_element_type=F32)
                dks[pl.ds(half * NB + 2 * j, 2)] = (dk * SCALE).astype(BF16).reshape(2, KP, DH)
                dvs[pl.ds(half * NB + 2 * j, 2)] = dv.astype(BF16).reshape(2, KP, DH)
                for step in (2 * e + 1, 2 * e):
                    if step not in HELD:
                        ship(half, step)

    def lead(i, carry):
        forward(2 * i)
        forward(2 * i + 1)
        send_stats(i)
        return carry

    def steady(i, carry):
        lead(i, carry)
        return rest(i - LAG, carry)

    def rest(i, carry):
        settle(sr.at[i], st_recv.at[i])
        backward(i, 0)
        backward(i, 1)
        return carry

    dka[...] = jnp.zeros_like(dka)
    dva[...] = jnp.zeros_like(dva)
    settle(kb.at[0], l_sem.at[0])
    settle(vb.at[0], l_sem.at[1])
    settle_in(0)
    state = score(0, 0, fresh())
    pl.semaphore_wait(barrier, 2 * NB + NG - 2)

    mate = 2 * p + 1 - c
    remote(k_hbm.at[:, cols(mate)], kb.at[1], kv_send, kv_recv, p, m ^ 1)
    remote(v_hbm.at[:, cols(mate)], vb.at[1], kv_send, kv_recv, p, m ^ 1)
    for i in range(1, NB):
        to = p ^ ORDER[i]
        remote(q_hbm.at[:, cols(2 * to + c)], qb.at[i], in_send.at[0], in_recv.at[i, 0], to, m)
        remote(do_hbm.at[:, cols(2 * to + c)], dob.at[i], in_send.at[1], in_recv.at[i, 1], to, m)

    kt[0] = kb[0].T
    settle(kb, kv_recv)
    finish(0, score(0, 1, state))
    forward(1)
    send_stats(0)
    kt[1] = kb[1].T
    lax.fori_loop(1, LAG, lead, 0)
    lax.fori_loop(LAG, NB // 2, steady, 0)
    lax.fori_loop(NB // 2 - LAG, NB // 2 - 1, rest, 0)
    for batch in range(EARLY):
        finals(batch)
    settle(sr.at[NB // 2 - 1], st_recv.at[NB // 2 - 1])
    backward_last()
    for batch in range(EARLY, NB // BATCH):
        finals(batch)
    for step in HELD:
        for half in (1, 0):
            ship(half, step)

    settle(kb, kv_send)
    settle(qb.at[1:], in_send.at[0])
    settle(dob.at[1:], in_send.at[1])
    settle(sr.at[:, 1:], st_send)
    settle(dqs.at[:, 1:], dq_send)
    settle(dqo.at[1:], f_send)
    settle(dks.at[1:], o_send.at[0])
    settle(dvs.at[1:], o_send.at[1])
    settle(dq_out, f_recv)
    settle(dk_out, o_recv.at[0])
    settle(dv_out, o_recv.at[1])


def place(dq, dk, dv, dq_out, dk_out, dv_out, dqv, dkv, dvv, in_sem, out_sem):
    steps = [(dq, dqv, dq_out)]
    for n in range(2):
        rows = pl.ds(n * KP // 2, KP // 2)
        for src, via, dst in ((dk, dkv, dk_out.at[0]), (dv, dvv, dv_out.at[0])):
            steps.append((src.at[rows], via.at[rows], dst.at[rows]))
    fetch = [pltpu.make_async_copy(src, via, in_sem.at[i]) for i, (src, via, _) in enumerate(steps)]
    store = [pltpu.make_async_copy(via, dst, out_sem.at[i]) for i, (_, via, dst) in enumerate(steps)]
    for copy in fetch:
        copy.start()
    for first, second in zip(fetch, store):
        first.wait()
        second.start()
    for copy in store:
        copy.wait()


def shards(queries, keys, values, d_out):
    width = queries.shape[1]
    dma = pltpu.SemaphoreType.DMA
    any_space = pl.BlockSpec(memory_space=pl.ANY)
    dq, dk, dv = pl.pallas_call(
        kernel,
        out_shape=(
            jax.ShapeDtypeStruct((8, width), F32),
            jax.ShapeDtypeStruct((KP, width), BF16),
            jax.ShapeDtypeStruct((KP, width), BF16),
        ),
        in_specs=[any_space] * 4,
        out_specs=[any_space] * 3,
        scratch_shapes=[
            pltpu.VMEM((NB, RB, DH), BF16),
            pltpu.VMEM((NB, RB, DH), BF16),
            pltpu.VMEM((2, KB, DH), BF16),
            pltpu.VMEM((2, KB, DH), BF16),
            pltpu.VMEM((2, DH, KB), BF16),
            pltpu.VMEM((NB, 2, KB, RB), F32),
            pltpu.VMEM((NB, 2, KB, RB), F32),
            pltpu.VMEM((NB, 8, 128), F32),
            pltpu.VMEM((NB // 2, NG, 2, 8, 128), F32),
            pltpu.VMEM((2, KB, 2 * RB), BF16),
            pltpu.VMEM((2, KB, 2 * RB), BF16),
            pltpu.VMEM((2, KB, DH), F32),
            pltpu.VMEM((2, KB, DH), F32),
            pltpu.VMEM((2 * NB, KP, DH), BF16),
            pltpu.VMEM((2 * NB, KP, DH), BF16),
            pltpu.VMEM((NB // BATCH, NG, BATCH, RB // NG, DH), BF16),
            pltpu.VMEM((NB // BATCH, NG, BATCH, RB // NG, DH), BF16),
            pltpu.VMEM((2 * NB, 8, DH), F32),
            dma((2,)),
            dma,
            dma,
            dma((2,)),
            dma((NB, 2)),
            dma,
            dma((NB // 2,)),
            dma((2,)),
            dma((2,)),
            dma,
            dma((NB // BATCH,)),
            dma,
            dma,
        ],
        compiler_params=pltpu.CompilerParams(
            collective_id=0, has_side_effects=True, vmem_limit_bytes=56 * 2**20
        ),
        cost_estimate=pl.CostEstimate(flops=5 * 2 * 2048 * 2048 * 128, bytes_accessed=12 * 2**20, transcendentals=2 * 2048 * 2048),
    )(queries, keys, values, d_out)
    return pl.pallas_call(
        place,
        out_shape=(
            jax.ShapeDtypeStruct((8, width), F32),
            jax.ShapeDtypeStruct((1, KP, width), BF16),
            jax.ShapeDtypeStruct((1, KP, width), BF16),
        ),
        in_specs=[any_space] * 3,
        out_specs=[any_space] * 3,
        scratch_shapes=[
            pltpu.VMEM((8, width), F32),
            pltpu.VMEM((KP, width), BF16),
            pltpu.VMEM((KP, width), BF16),
            dma((5,)),
            dma((5,)),
        ],
    )(dq, dk, dv)


def solution(mesh):
    return jax.shard_map(
        shards,
        mesh=mesh,
        in_specs=(P("pb", None), P("mem", None), P("mem", None), P("pb", None)),
        out_specs=(P(("pb", "mem"), None), P("mem", "pb", None), P("mem", "pb", None)),
        check_vma=False,
    )
```
